32 devices in a mesh: groups: 2 (over y), ctx: 4 (over x, core), head: 4 (over z).
Axes of the slice: x: 2, y: 2, z: 4, core: 2. Of those that a mesh axis runs over, the one named last changes fastest.
Arguments:
- attn_out: bfloat16 [1024, 8192], P(('groups', 'ctx'), 'head'), parts along dimension 0, may hold values from -6 to 6
- out_weight: bfloat16 [8192, 7168], P('head', 'ctx'), may hold values from -0.0625 to 0.0625
- residual: bfloat16 [1024, 7168], P(('groups', 'ctx', 'head')), parts along dimension 0, may hold values from -6 to 6
- norm_gain: float32 [7168], replicated, may hold values from 0.1 to 1.9
- expert_ids: int32 [1024, 2], P(('groups', 'ctx', 'head')), parts along dimension 0, may hold values from 0 to 3, all different within a row; in each aligned block of 32 rows (0 to 31, 32 to 63, ...) at most 24 rows name the same one
- gate_codes: int32 [1024, 2], P(('groups', 'ctx', 'head')), parts along dimension 0, may hold values from 1 to 1024
- w_gate: bfloat16 [4, 7168, 2048], P('ctx', None, 'head'), may hold values from -0.0625 to 0.0625
- w_up: bfloat16 [4, 7168, 2048], P('ctx', None, 'head'), may hold values from -0.0625 to 0.0625
- w_down: bfloat16 [4, 2048, 7168], P('ctx', 'head'), may hold values from -0.125 to 0.125
Outputs:
- mixed: bfloat16 [1024, 7168], P(('groups', 'ctx', 'head')), parts along dimension 0
The draws below stay inside these ranges and needn't reach their ends.
There are 2 independent parts, one for each index of `groups`. The reference program is written for one: setup_inputs(seed, part) draws one part's arguments, and reference() takes and returns one part's arrays. A program takes and returns all parts, laid end to end along the dimension named above; an argument that names none is the same for every part. Nothing has to cross between parts.
Inputs may be any that keep to these rules, and one draw needn't show every extreme that they name: `expert_ids`: each row names 2 different experts. In each aligned block of 32 rows no expert is named by more than 24 rows, a bound that some block reaches.
All inputs are finite; a program needn't handle non-finite values.
Results may differ from the reference program's by a relative error of at most 0.017.
Values may be sent and summed in bfloat16 or wider, within the bound.
A program may use at most 128 MiB of HBM per device.

```python
import math
import jax
import jax.numpy as jnp
import numpy as np
from jax import lax

D = 7168
HEADS = 64
DV = 128
FF = 2048
ROUTES = 2
TOKENS = 512
ROWS_DEV = 32
EXPERTS = 4
CAP = 24
N_HEAD = 4


def touch_ends(result, key, least, top_value):
    index_at = [jax.random.randint(jax.random.fold_in(key, axis), (), 0, length) for axis, length in enumerate(result.shape)]
    longest = result.shape.index(max(result.shape))
    beside = index_at[:longest] + [(index_at[longest] + 1) % result.shape[longest]] + index_at[longest + 1:]
    return result.at[tuple(index_at)].set(least).at[tuple(beside)].set(top_value)


def block_scale(own_key, shape, cuts, low, top_value):
    factor_of, own = 1.0, jax.random.fold_in(own_key, 6)
    for axis_at, parts in cuts:
        heights = jnp.exp(jax.random.uniform(jax.random.fold_in(own, axis_at), (parts,), jnp.float32, low / len(cuts), top_value / len(cuts)))
        factor_of = factor_of * jnp.repeat(heights, shape[axis_at] // parts).reshape([-1 if axis == axis_at else 1 for axis in range(len(shape))])
    return factor_of


def shared_out(stream_key, own, number, rows, number_of, top, reach, skew):
    order = jax.random.permutation(stream_key, number_of)
    heavy_load, usual = portions_of(number_of, rows * top, reach, skew, True), portions_of(number_of, rows * top, reach, skew, False)
    places = jnp.arange(number_of)

    def named(sizes, rotation):
        used = int((sizes > 0).sum())
        fixed = max(1, used // 4)
        passed = fixed + (places - fixed + rotation * (used - fixed)) % max(1, number_of - fixed)
        return jnp.zeros((number_of,), jnp.int32).at[order[jnp.where(places < fixed, places, passed)]].set(jnp.asarray(sizes, jnp.int32))

    sizes = jnp.where(number % 4 == 0, named(heavy_load, number // 4), named(usual, number - number // 4 - 1))
    mixed = jax.random.permutation(jax.random.fold_in(own, 3), number_of)
    donor, receiver = mixed[0:number_of // 2 * 2:2], mixed[1:number_of // 2 * 2:2]
    room = jnp.minimum(sizes[donor] - 1, reach - sizes[receiver]) // 2
    room = jnp.where((donor == order[0]) | (receiver == order[0]) | (sizes[receiver] == 0), 0, jnp.maximum(room, 0))
    passed = jax.random.randint(jax.random.fold_in(own, 4), (number_of // 2,), 0, 1 << 20) % (room + 1)
    sizes = sizes.at[donor].add(-passed).at[receiver].add(passed)
    members = jnp.searchsorted(jnp.cumsum(sizes), jnp.arange(rows * top), side="right").astype(jnp.int32)
    table = members.reshape(top, rows).T
    table = table[jax.random.permutation(jax.random.fold_in(own, 1), rows)]
    rotation = jax.random.randint(jax.random.fold_in(own, 2), (rows, 1), 0, top)
    return jnp.take_along_axis(table, (jnp.arange(top)[None, :] + rotation) % top, axis=1)


def portions_of(amount, total, bound, lean, full):
    weights = [(1 << 20) // math.isqrt(standing ** lean) + 1 for standing in range(1, amount + 1)]
    largest = bound if full else min(bound, max(-(-total // amount), total * weights[0] // sum(weights)))
    least = 1 if total - largest >= amount - 1 else 0
    given, surplus = [largest] + [least] * (amount - 1), total - largest - least * (amount - 1)
    while surplus > 0:
        candidates = [i for i in range(1, amount) if given[i] < largest] or [i for i in range(1, amount) if given[i] < bound]
        pool, budget = sum([weights[i] for i in candidates]), surplus
        for i in candidates:
            addition = min(bound - given[i], max(1, budget * weights[i] // pool), surplus)
            given[i] = given[i] + addition
            surplus = surplus - addition
    return np.array(given)


def bell_draw(own_key, extent, spread, bound, cuts=(), kind=jnp.bfloat16):
    drawn = spread * jax.random.normal(own_key, extent, jnp.float32)
    if cuts:
        drawn = drawn * block_scale(own_key, extent, cuts, -0.22, 0.18)
    return jnp.clip(drawn, -bound, bound).astype(kind)


def setup_inputs(seed: int = 0, part: int = 0) -> dict:
    key_of = jax.random.split(jax.random.key(seed), 10)
    part_splits = jax.random.split(jax.random.fold_in(key_of[9], part), 10)
    attn_out = bell_draw(part_splits[0], (TOKENS, HEADS * DV), 1.0, 6.0, ((0, 4), (1, 4)))
    out_weight = bell_draw(key_of[1], (HEADS * DV, D), (HEADS * DV) ** -0.5, 0.0625, ((0, 4), (1, 4)))
    residual = bell_draw(part_splits[2], (TOKENS, D), 1.0, 6.0, ((0, 16),))
    norm_gain = jnp.clip(1.0 + 0.18 * jax.random.normal(key_of[3], (D,), jnp.float32), 0.1, 1.9)
    expert_ids_keys = jax.random.split(jax.random.fold_in(part_splits[4], 1), TOKENS // ROWS_DEV)
    expert_ids_turns = jax.random.permutation(jax.random.fold_in(part_splits[4], 3), TOKENS // ROWS_DEV)
    expert_ids = jax.vmap(lambda own, number: shared_out(jax.random.fold_in(part_splits[4], 2), own, number, ROWS_DEV, EXPERTS, ROUTES, CAP, 2))(expert_ids_keys, expert_ids_turns).reshape((TOKENS, ROUTES))
    gate_codes = touch_ends(jax.random.randint(part_splits[5], (TOKENS, ROUTES), 1, 1025), jax.random.fold_in(part_splits[5], 1), 1, 1024).astype(jnp.int32)
    w_gate = bell_draw(key_of[6], (EXPERTS, D, FF), D ** -0.5, 0.0625, ((0, 4), (2, 4)))
    w_up = bell_draw(key_of[7], (EXPERTS, D, FF), D ** -0.5, 0.0625, ((0, 4), (2, 4)))
    w_down = bell_draw(key_of[8], (EXPERTS, FF, D), FF ** -0.5, 0.125, ((0, 4), (1, 4)))
    return dict(attn_out=attn_out, out_weight=out_weight, residual=residual, norm_gain=norm_gain, expert_ids=expert_ids, gate_codes=gate_codes, w_gate=w_gate, w_up=w_up, w_down=w_down)


def reference(attn_out, out_weight, residual, norm_gain, expert_ids, gate_codes, w_gate, w_up, w_down):
    projected = jnp.dot(attn_out, out_weight, preferred_element_type=jnp.float32)
    hidden_state = residual.astype(jnp.float32) + projected
    mean_square = lax.optimization_barrier(jnp.mean(hidden_state * hidden_state, axis=1, keepdims=True))
    normed = (hidden_state * lax.rsqrt(mean_square + 1e-06) * norm_gain).astype(jnp.bfloat16)
    gate_values = gate_codes.astype(jnp.float32)
    route_weights = 2.5 * gate_values / lax.optimization_barrier(jnp.sum(gate_values, axis=1, keepdims=True))
    blocks = TOKENS // ROWS_DEV
    flat_ids = expert_ids.reshape(blocks, ROWS_DEV * ROUTES)
    onehot = (flat_ids[:, :, None] == jnp.arange(EXPERTS, dtype=jnp.int32)[None, None, :]).astype(jnp.int32)
    before = jnp.cumsum(onehot, axis=1) - onehot
    slot_index = lax.optimization_barrier(jnp.sum(onehot * before, axis=2))
    block_index = jnp.arange(blocks, dtype=jnp.int32)[:, None]
    places = (block_index * CAP + slot_index).reshape(-1).astype(jnp.int32)
    token_of = (block_index * ROWS_DEV + jnp.arange(ROWS_DEV * ROUTES, dtype=jnp.int32)[None, :] // ROUTES).reshape(-1).astype(jnp.int32)
    route_ids = flat_ids.reshape(-1)
    flat_weights = route_weights.reshape(-1)
    shard_width = FF // N_HEAD
    token_rows = normed[token_of]

    def one_expert(combined, expert):
        chosen = route_ids == expert
        target = jnp.where(chosen, places, blocks * CAP).astype(jnp.int32)
        buffer = jnp.zeros((blocks * CAP, D), jnp.bfloat16).at[target].set(token_rows, mode='drop')
        gate_proj = jnp.dot(buffer, w_gate[expert], preferred_element_type=jnp.float32)
        up_proj = jnp.dot(buffer, w_up[expert], preferred_element_type=jnp.float32)
        activation = (jax.nn.silu(gate_proj) * up_proj).astype(jnp.bfloat16)
        down_rows = w_down[expert]
        output = jnp.zeros((blocks * CAP, D), jnp.float32)
        for part_index in range(N_HEAD):
            lower = part_index * shard_width
            term = jnp.dot(activation[:, lower:lower + shard_width], down_rows[lower:lower + shard_width], preferred_element_type=jnp.float32).astype(jnp.bfloat16)
            term = lax.optimization_barrier(term)
            output = output + term.astype(jnp.float32)
        gathered = output[places]
        scaled = jnp.where(chosen, flat_weights, jnp.zeros_like(flat_weights))[:, None] * gathered
        combined = combined.at[token_of].add(scaled)
        return (combined, None)
    combined, unused = lax.scan(one_expert, jnp.zeros((TOKENS, D), jnp.float32), jnp.arange(EXPERTS, dtype=jnp.int32))
    return (hidden_state + combined).astype(jnp.bfloat16)
```

```python
import jax
import jax.numpy as jnp
from jax import lax
from jax.sharding import PartitionSpec as P


def route_places(expert_ids, experts, capacity):
    flattened = expert_ids.reshape(-1)
    onehot = (flattened[:, None] == jnp.arange(experts, dtype=jnp.int32)[None, :]).astype(jnp.int32)
    before = jnp.cumsum(onehot, axis=0) - onehot
    slot_index = jnp.sum(onehot * before, axis=1)
    return (flattened * capacity + slot_index).reshape(expert_ids.shape)


def expert_apply(token_rows, w_gate, w_up, w_down):
    row_shape = token_rows.shape
    flattened = token_rows.reshape(-1, row_shape[-1])
    gate_proj = jnp.dot(flattened, w_gate[0], preferred_element_type=jnp.float32)
    up_proj = jnp.dot(flattened, w_up[0], preferred_element_type=jnp.float32)
    activation = (jax.nn.silu(gate_proj) * up_proj).astype(jnp.bfloat16)
    result = jnp.dot(activation, w_down[0], preferred_element_type=jnp.float32)
    return result.reshape(row_shape)


def local(attn_out, out_weight, residual, norm_gain, expert_ids, gate_codes, w_gate, w_up, w_down):
    ctx_count = lax.axis_size("ctx")
    rows_dev = residual.shape[0]
    model_width = residual.shape[1]
    partial_sums = jnp.dot(
        attn_out,
        lax.all_gather(out_weight, "ctx", axis=1, tiled=True),
        preferred_element_type=jnp.float32,
    )
    projected = lax.psum_scatter(
        partial_sums.astype(jnp.bfloat16), "head", scatter_dimension=0, tiled=True
    ).astype(jnp.float32)
    hidden_state = residual.astype(jnp.float32) + projected
    mean_square = jnp.mean(hidden_state * hidden_state, axis=1, keepdims=True)
    normed = (hidden_state * lax.rsqrt(mean_square + 1e-06) * norm_gain).astype(jnp.bfloat16)
    routes = expert_ids.shape[1]
    capacity = min(rows_dev, max(2, (3 * rows_dev * routes + 2 * ctx_count - 1) // (2 * ctx_count)))
    places = route_places(expert_ids, ctx_count, capacity)
    slot_range = jnp.arange(ctx_count * capacity, dtype=jnp.int32)
    select = jnp.any(slot_range[:, None, None] == places[None, :, :], axis=2).astype(jnp.bfloat16)
    outbound = jnp.dot(select, normed, preferred_element_type=jnp.float32).astype(jnp.bfloat16)
    outbound = outbound.reshape(ctx_count, capacity, model_width)
    arrived = lax.all_to_all(outbound, "ctx", split_axis=0, concat_axis=0, tiled=True)
    partial_out = expert_apply(
        lax.all_gather(arrived[:, None], "head", axis=1, tiled=True), w_gate, w_up, w_down
    )
    summed_out = lax.psum_scatter(
        partial_out.astype(jnp.bfloat16), "head", scatter_dimension=1, tiled=True
    ).astype(jnp.float32)
    returned = lax.all_to_all(
        summed_out.reshape(ctx_count, capacity, model_width).astype(jnp.bfloat16),
        "ctx",
        split_axis=0,
        concat_axis=0,
        tiled=True,
    ).astype(jnp.float32)
    gate_values = gate_codes.astype(jnp.float32)
    route_weights = 2.5 * gate_values / jnp.sum(gate_values, axis=1, keepdims=True)
    matching = places[:, :, None] == slot_range[None, None, :]
    mixing = jnp.sum(jnp.where(matching, route_weights[:, :, None], 0.0), axis=1)
    combined = jnp.dot(
        mixing,
        returned.reshape(ctx_count * capacity, model_width),
        precision=lax.Precision.HIGHEST,
        preferred_element_type=jnp.float32,
    )
    return (hidden_state + combined).astype(jnp.bfloat16)


def local_dense(attn_out, out_weight, residual, norm_gain, expert_ids, gate_codes, w_gate, w_up, w_down):
    ctx_count, head_count = lax.axis_size("ctx"), lax.axis_size("head")
    rows_dev, model_width = residual.shape
    expert = lax.axis_index("ctx")
    attn = lax.all_gather(attn_out, "ctx", axis=0, tiled=True)
    partial = jnp.dot(attn, out_weight, preferred_element_type=jnp.float32).astype(jnp.bfloat16)
    partial = partial.reshape(ctx_count, head_count, rows_dev, -1).transpose(1, 0, 2, 3)
    partial = partial.reshape(head_count * ctx_count * rows_dev, -1)
    summed = lax.psum_scatter(partial, "head", scatter_dimension=0, tiled=True)
    summed = summed.reshape(ctx_count, rows_dev, -1)
    projected = lax.all_to_all(summed, "ctx", split_axis=0, concat_axis=2, tiled=True)
    hidden_state = residual.astype(jnp.float32) + projected.reshape(rows_dev, model_width).astype(jnp.float32)
    mean_square = jnp.mean(hidden_state * hidden_state, axis=1, keepdims=True)
    normed = (hidden_state * lax.rsqrt(mean_square + 1e-06) * norm_gain).astype(jnp.bfloat16)
    gate_values = gate_codes.astype(jnp.float32)
    route_weights = 2.5 * gate_values / jnp.sum(gate_values, axis=1, keepdims=True)
    named = expert_ids[:, :, None] == jnp.arange(ctx_count, dtype=jnp.int32)
    weights = jnp.sum(jnp.where(named, route_weights[:, :, None], 0.0), axis=1)
    weights = lax.all_gather(weights, ("ctx", "head"), axis=0, tiled=True)
    mine = jnp.sum(jnp.where(jnp.arange(ctx_count) == expert, weights, 0.0), axis=1, keepdims=True)
    rows = lax.all_gather(normed, ("ctx", "head"), axis=0, tiled=True)
    gate_proj = jnp.dot(rows, w_gate[0], preferred_element_type=jnp.float32)
    up_proj = jnp.dot(rows, w_up[0], preferred_element_type=jnp.float32)
    activation = (jax.nn.silu(gate_proj) * up_proj).astype(jnp.bfloat16)
    out = jnp.dot(activation, w_down[0], preferred_element_type=jnp.float32)
    out = jnp.where(mine == 0.0, 0.0, out * mine).astype(jnp.bfloat16)
    combined = lax.psum_scatter(out, ("ctx", "head"), scatter_dimension=0, tiled=True)
    return (hidden_state + combined.astype(jnp.float32)).astype(jnp.bfloat16)


def solution(mesh):
    in_specs = (
        P(("groups", "ctx"), "head"),
        P("head", "ctx"),
        P(("groups", "ctx", "head"), None),
        P(),
        P(("groups", "ctx", "head"), None),
        P(("groups", "ctx", "head"), None),
        P("ctx", None, "head"),
        P("ctx", None, "head"),
        P("ctx", "head", None),
    )
    out_specs = P(("groups", "ctx", "head"), None)
    dense = 2 * mesh.shape["ctx"] <= 8
    body = local_dense if dense else local
    return jax.shard_map(body, mesh=mesh, in_specs=in_specs, out_specs=out_specs, check_vma=False)
```

```python
import jax
import jax.numpy as jnp
from jax import lax
from jax.experimental import pallas as pl
from jax.experimental.pallas import tpu as pltpu
from jax.sharding import PartitionSpec as P


def route_places(expert_ids, experts, capacity):
    flattened = expert_ids.reshape(-1)
    onehot = (flattened[:, None] == jnp.arange(experts, dtype=jnp.int32)[None, :]).astype(jnp.int32)
    before = jnp.cumsum(onehot, axis=0) - onehot
    slot_index = jnp.sum(onehot * before, axis=1)
    return (flattened * capacity + slot_index).reshape(expert_ids.shape)


def expert_apply(token_rows, w_gate, w_up, w_down):
    row_shape = token_rows.shape
    flattened = token_rows.reshape(-1, row_shape[-1])
    gate_proj = jnp.dot(flattened, w_gate[0], preferred_element_type=jnp.float32)
    up_proj = jnp.dot(flattened, w_up[0], preferred_element_type=jnp.float32)
    activation = (jax.nn.silu(gate_proj) * up_proj).astype(jnp.bfloat16)
    result = jnp.dot(activation, w_down[0], preferred_element_type=jnp.float32)
    return result.reshape(row_shape)


def local(attn_out, out_weight, residual, norm_gain, expert_ids, gate_codes, w_gate, w_up, w_down):
    ctx_count = lax.axis_size("ctx")
    rows_dev = residual.shape[0]
    model_width = residual.shape[1]
    partial_sums = jnp.dot(
        attn_out,
        lax.all_gather(out_weight, "ctx", axis=1, tiled=True),
        preferred_element_type=jnp.float32,
    )
    projected = lax.psum_scatter(
        partial_sums.astype(jnp.bfloat16), "head", scatter_dimension=0, tiled=True
    ).astype(jnp.float32)
    hidden_state = residual.astype(jnp.float32) + projected
    mean_square = jnp.mean(hidden_state * hidden_state, axis=1, keepdims=True)
    normed = (hidden_state * lax.rsqrt(mean_square + 1e-06) * norm_gain).astype(jnp.bfloat16)
    routes = expert_ids.shape[1]
    capacity = min(rows_dev, max(2, (3 * rows_dev * routes + 2 * ctx_count - 1) // (2 * ctx_count)))
    places = route_places(expert_ids, ctx_count, capacity)
    slot_range = jnp.arange(ctx_count * capacity, dtype=jnp.int32)
    select = jnp.any(slot_range[:, None, None] == places[None, :, :], axis=2).astype(jnp.bfloat16)
    outbound = jnp.dot(select, normed, preferred_element_type=jnp.float32).astype(jnp.bfloat16)
    outbound = outbound.reshape(ctx_count, capacity, model_width)
    arrived = lax.all_to_all(outbound, "ctx", split_axis=0, concat_axis=0, tiled=True)
    partial_out = expert_apply(
        lax.all_gather(arrived[:, None], "head", axis=1, tiled=True), w_gate, w_up, w_down
    )
    summed_out = lax.psum_scatter(
        partial_out.astype(jnp.bfloat16), "head", scatter_dimension=1, tiled=True
    ).astype(jnp.float32)
    returned = lax.all_to_all(
        summed_out.reshape(ctx_count, capacity, model_width).astype(jnp.bfloat16),
        "ctx",
        split_axis=0,
        concat_axis=0,
        tiled=True,
    ).astype(jnp.float32)
    gate_values = gate_codes.astype(jnp.float32)
    route_weights = 2.5 * gate_values / jnp.sum(gate_values, axis=1, keepdims=True)
    matching = places[:, :, None] == slot_range[None, None, :]
    mixing = jnp.sum(jnp.where(matching, route_weights[:, :, None], 0.0), axis=1)
    combined = jnp.dot(
        mixing,
        returned.reshape(ctx_count * capacity, model_width),
        precision=lax.Precision.HIGHEST,
        preferred_element_type=jnp.float32,
    )
    return (hidden_state + combined).astype(jnp.bfloat16)


BF16, F32 = jnp.bfloat16, jnp.float32
SEMS = 72


def layer_kernel(
    attn, out_w, resid, gain, route_w, gate_w, up_w, down_w, out,
    attn_all, work, gate_v, up_v, down_v, res_cols, part, arrived, hidden, scaled,
    gate_acc, up_acc, square_sum, act, route_all, mine,
    core_in, core_x_in, head_in, last_out, last_in, send, recv, local_sem,
):
    c, h = lax.axis_index("ctx"), lax.axis_index("head")
    x, k = c // 2, c % 2
    rows = resid.shape[0]
    span, group = 4 * rows, 16 * rows
    cols = part.shape[2]
    tile = 256 if cols % 256 == 0 else 128
    tiles = cols // tile
    hidden_units = gate_acc.shape[1]

    ctx_of = [c, 2 * x + (1 - k), 2 * (1 - x) + k, 2 * (1 - x) + (1 - k)]
    to = [lax.rem(h + d, 4) for d in range(4)]
    source = [lax.rem(h + 4 - d, 4) for d in range(4)]
    SIB, ACROSS, DIAG = 1, 2, 3

    def at(start, size):
        return pl.ds(pl.multiple_of(start, size), size)

    def cols_at(start):
        return pl.ds(pl.multiple_of(start, 128), tile)

    def remote(src, dst, number, j=0, d=0, back=False):
        head = (source if back else to)[d]
        return pltpu.make_async_remote_copy(
            src_ref=src, dst_ref=dst, send_sem=send.at[number], recv_sem=recv.at[number],
            device_id={"ctx": ctx_of[j], "head": head}, device_id_type=pl.DeviceIdType.MESH,
        )

    started = []

    def push(src, dst, number, j=0, d=0):
        copy = remote(src, dst, number, j, d)
        copy.start()
        started.append(copy)

    def landed(dst, number, j=0, d=0):
        remote(dst, dst, number, j, d, back=True).wait_recv()

    barrier = pltpu.get_barrier_semaphore()
    for j in range(4):
        for d in range(4):
            if (j, d) != (0, 0):
                pl.semaphore_signal(
                    barrier, inc=1, device_id={"ctx": ctx_of[j], "head": to[d]},
                    device_id_type=pl.DeviceIdType.MESH,
                )

    depth = out_w.shape[0]
    own_copies = [
        pltpu.make_async_copy(attn, attn_all.at[c], local_sem.at[0]),
        pltpu.make_async_copy(out_w, work.at[pl.ds(0, depth)], local_sem.at[1]),
        pltpu.make_async_copy(resid.at[:, at(c * cols, cols)], res_cols.at[at(c * rows, rows)], local_sem.at[2]),
        pltpu.make_async_copy(gate_w.at[0], gate_v, local_sem.at[3]),
        pltpu.make_async_copy(up_w.at[0], up_v, local_sem.at[4]),
        pltpu.make_async_copy(down_w.at[0], down_v, local_sem.at[5]),
    ]
    for copy in own_copies:
        copy.start()
    pl.semaphore_wait(barrier, 15)

    push(attn, attn_all.at[c], 0, ACROSS)
    push(attn, attn_all.at[c], 1, SIB)
    for j in (1, 2, 3):
        push(resid.at[:, at(ctx_of[j] * cols, cols)], res_cols.at[at(c * rows, rows)], 2 + j, j)
    for j in range(4):
        for d in range(4):
            if (j, d) != (0, 0):
                push(route_w, route_all.at[at(h * span + c * rows, rows)], 6 + 4 * j + d - 1, j, d)
    route_all[at(h * span + c * rows, rows), :] = route_w[...]

    def project(j):
        block = ctx_of[j]

        def step(t, _):
            column = cols_at(t * tile)
            y = jnp.dot(attn_all[block], work[pl.ds(0, depth), column], preferred_element_type=F32).astype(BF16)
            for i in range(4):
                part[i, at(block * rows, rows), column] = y[i * rows:(i + 1) * rows]
            return 0

        lax.fori_loop(0, tiles, step, 0)
        for d in (2, 1, 3):
            place = at(block * rows, rows)
            push(part.at[to[d], place], arrived.at[d - 1, place], 21 + 3 * j + d - 1, 0, d)

    own_copies[0].wait()
    own_copies[1].wait()
    project(0)
    landed(attn_all.at[ctx_of[SIB]], 1, SIB)
    project(1)
    landed(attn_all.at[ctx_of[ACROSS]], 0, ACROSS)
    push(attn_all.at[ctx_of[ACROSS]], attn_all.at[ctx_of[ACROSS]], 2, SIB)
    project(2)
    landed(attn_all.at[ctx_of[DIAG]], 2, SIB)
    project(3)

    own_copies[2].wait()
    for j in (1, 2, 3):
        landed(res_cols.at[at(ctx_of[j] * rows, rows)], 2 + j, j)
    for j in range(4):
        for d in (1, 2, 3):
            landed(arrived.at[d - 1, at(ctx_of[j] * rows, rows)], 21 + 3 * j + d - 1, 0, d)

    def add_up(t, _):
        column = cols_at(t * tile)
        total = part[h, :, column].astype(F32) + res_cols[:, column].astype(F32)
        for d in range(3):
            total = total + arrived[d, :, column].astype(F32)
        hidden[c, at(h * span, span), column] = total.astype(BF16)
        return 0

    lax.fori_loop(0, tiles, add_up, 0)

    def block_of(j, d):
        return hidden.at[ctx_of[j], at(source[d] * span, span)]

    for d in (2, 1, 3):
        push(block_of(0, 0), block_of(0, 0), 33 + d - 1, 0, d)
    push(block_of(0, 0), block_of(0, 0), 36, ACROSS)
    push(block_of(0, 0), block_of(0, 0), 40, SIB)

    square_sum[...] = jnp.zeros_like(square_sum)
    gate_acc[...] = jnp.zeros_like(gate_acc)
    up_acc[...] = jnp.zeros_like(up_acc)
    for j in range(4):
        for d in range(4):
            if (j, d) != (0, 0):
                landed(route_all.at[at(source[d] * span + ctx_of[j] * rows, rows)], 6 + 4 * j + d - 1, j, d)
    lane = lax.broadcasted_iota(jnp.int32, route_all.shape, 1)
    mine[...] = jnp.sum(jnp.where(lane == c, route_all[...], 0.0), axis=1, keepdims=True)

    def expand(j):
        block = ctx_of[j]

        def scale(i, _):
            column = lax.rem(i, tiles)
            place = at((i // tiles) * span, span)
            value = hidden[block, place, cols_at(column * tile)].astype(F32)
            square_sum[place, :] += jnp.sum(value * value, axis=1, keepdims=True)
            g = gain[:, cols_at(block * cols + column * tile)]
            scaled[place, cols_at(column * tile)] = (value * g).astype(BF16)
            return 0

        lax.fori_loop(0, 4 * tiles, scale, 0)

        def step(t, _):
            unit = cols_at(t * tile)
            place = at(block * cols, cols)
            gate_acc[:, unit] += jnp.dot(scaled[...], gate_v[place, unit], preferred_element_type=F32)
            up_acc[:, unit] += jnp.dot(scaled[...], up_v[place, unit], preferred_element_type=F32)
            return 0

        lax.fori_loop(0, hidden_units // tile, step, 0)

    for d in (1, 3, 2):
        landed(block_of(0, d), 33 + d - 1, 0, d)
        push(block_of(0, d), block_of(0, d), 36 + d, ACROSS)
        push(block_of(0, d), block_of(0, d), 40 + d, SIB)
    landed(block_of(ACROSS, 0), 36, ACROSS)
    push(block_of(ACROSS, 0), block_of(ACROSS, 0), 44, SIB)
    own_copies[3].wait()
    own_copies[4].wait()
    expand(0)
    for d in (1, 3):
        landed(block_of(ACROSS, d), 36 + d, ACROSS)
        push(block_of(ACROSS, d), block_of(ACROSS, d), 44 + d, SIB)
    for d in range(4):
        landed(block_of(SIB, d), 40 + d, SIB)
    expand(1)
    landed(block_of(ACROSS, 2), 38, ACROSS)
    push(block_of(ACROSS, 2), block_of(ACROSS, 2), 46, SIB)
    expand(2)
    for d in range(4):
        landed(block_of(DIAG, d), 44 + d, SIB)
    expand(3)

    def activate(i, _):
        place = at(i * rows, rows)
        r = lax.rsqrt(square_sum[place, :] * (1.0 / (4 * cols)) + 1e-06)
        g = gate_acc[place, :] * r
        act[place, :] = (g / (1.0 + jnp.exp(-g)) * (up_acc[place, :] * r)).astype(BF16)
        return 0

    lax.fori_loop(0, 16, activate, 0)
    own_copies[5].wait()

    def chunk(s, block):
        return (4 * s + block) * span

    def down(s):
        target = to[(s + 1) % 4]

        def step(i, _):
            block, t = i // tiles, lax.rem(i, tiles)
            y = jnp.dot(
                act[at(target * span, span), :], down_v[:, cols_at(block * cols + t * tile)],
                preferred_element_type=F32,
            )
            y = y * mine[at(target * span, span), :]
            work[at(chunk(s, block), span), cols_at(t * tile)] = y.astype(BF16)
            return 0

        lax.fori_loop(0, 4 * tiles, step, 0)
        push(work.at[pl.ds(pl.multiple_of(chunk(s, 2 * (1 - k)), span), 2 * span)],
             core_in.at[s], 48 + s, SIB)

    half = 2 * rows

    def over_x(s):
        landed(core_in.at[s], 48 + s, SIB)

        def step(i, _):
            j, t = i // tiles, lax.rem(i, tiles)
            place, column = at(chunk(s, 2 * k + j), span), cols_at(t * tile)
            y = work[place, column].astype(F32) + core_in[s, at(j * span, span), column].astype(F32)
            work[place, column] = y.astype(BF16)
            return 0

        lax.fori_loop(0, 2 * tiles, step, 0)
        for j in range(2):
            push(work.at[at(chunk(s, 2 * k + j) + (1 - x) * half, half)], core_x_in.at[s, j], 52 + 2 * s + j, ACROSS)

    def over_head(s):
        for j in range(2):
            landed(core_x_in.at[s, j], 52 + 2 * s + j, ACROSS)

        def step(i, _):
            j, t = i // tiles, lax.rem(i, tiles)
            place, column = at(chunk(s, 2 * k + j) + x * half, half), cols_at(t * tile)
            y = work[place, column].astype(F32) + core_x_in[s, j, :, column].astype(F32)
            work[place, column] = y.astype(BF16)
            return 0

        lax.fori_loop(0, 2 * tiles, step, 0)
        if s < 3:
            for j in range(2):
                push(work.at[at(chunk(s, 2 * k + j) + x * half, half)], head_in.at[s, j], 60 + 2 * s + j, 0, s + 1)

    for s in range(4):
        down(s)
        if s:
            over_x(s - 1)
    over_x(3)
    for s in range(4):
        over_head(s)
    for s in range(3):
        for j in range(2):
            landed(head_in.at[s, j], 60 + 2 * s + j, 0, s + 1)

    def total(core, i):
        j, t = i // tiles, lax.rem(i, tiles)
        column = cols_at(t * tile)
        y = work[at(chunk(3, 2 * k + j) + x * half + core * rows, rows), column].astype(F32)
        for s in range(3):
            y = y + head_in[s, j, at(core * rows, rows), column].astype(F32)
        return y

    def other(i, _):
        last_out[i // tiles, :, cols_at(lax.rem(i, tiles) * tile)] = total(1 - k, i).astype(BF16)
        return 0

    lax.fori_loop(0, 2 * tiles, other, 0)
    push(last_out, last_in, 66, SIB)

    def finish(block, i, y):
        t = lax.rem(i, tiles)
        kept = hidden[block, at(h * span + c * rows, rows), cols_at(t * tile)].astype(F32)
        out[:, cols_at(block * cols + t * tile)] = (kept + y).astype(BF16)

    def own(i, _):
        finish(2 * k + i // tiles, i, total(k, i))
        return 0

    lax.fori_loop(0, 2 * tiles, own, 0)
    landed(last_in, 66, SIB)

    def theirs(i, _):
        y = last_in[i // tiles, :, cols_at(lax.rem(i, tiles) * tile)].astype(F32)
        finish(2 * (1 - k) + i // tiles, i, y)
        return 0

    lax.fori_loop(0, 2 * tiles, theirs, 0)
    for copy in started:
        copy.wait_send()


def local_kernel(attn_out, out_weight, residual, norm_gain, expert_ids, gate_codes, w_gate, w_up, w_down):
    rows, width = residual.shape
    depth, cols = out_weight.shape
    units = w_gate.shape[2]
    gate_values = gate_codes.astype(F32)
    route_weights = 2.5 * gate_values / jnp.sum(gate_values, axis=1, keepdims=True)
    named = expert_ids[:, :, None] == jnp.arange(128, dtype=jnp.int32)
    weights = jnp.sum(jnp.where(named, route_weights[:, :, None], 0.0), axis=1)
    span, group = 4 * rows, 16 * rows
    vmem, hbm = pl.BlockSpec(memory_space=pltpu.VMEM), pl.BlockSpec(memory_space=pl.ANY)
    return pl.pallas_call(
        layer_kernel,
        out_shape=jax.ShapeDtypeStruct((rows, width), BF16),
        in_specs=[hbm, hbm, hbm, vmem, vmem, hbm, hbm, hbm],
        out_specs=vmem,
        scratch_shapes=[
            pltpu.VMEM((4, span, depth), BF16),
            pltpu.VMEM((max(depth, 16 * span), cols), BF16),
            pltpu.VMEM((width, units), BF16),
            pltpu.VMEM((width, units), BF16),
            pltpu.VMEM((units, width), BF16),
            pltpu.VMEM((span, cols), BF16),
            pltpu.VMEM((4, span, cols), BF16),
            pltpu.VMEM((3, span, cols), BF16),
            pltpu.VMEM((4, group, cols), BF16),
            pltpu.VMEM((group, cols), BF16),
            pltpu.VMEM((group, units), F32),
            pltpu.VMEM((group, units), F32),
            pltpu.VMEM((group, 1), F32),
            pltpu.VMEM((group, units), BF16),
            pltpu.VMEM((group, 128), F32),
            pltpu.VMEM((group, 1), F32),
            pltpu.VMEM((4, 2 * span, cols), BF16),
            pltpu.VMEM((4, 2, 2 * rows, cols), BF16),
            pltpu.VMEM((3, 2, 2 * rows, cols), BF16),
            pltpu.VMEM((2, rows, cols), BF16),
            pltpu.VMEM((2, rows, cols), BF16),
            pltpu.SemaphoreType.DMA((SEMS,)),
            pltpu.SemaphoreType.DMA((SEMS,)),
            pltpu.SemaphoreType.DMA((6,)),
        ],
        compiler_params=pltpu.CompilerParams(
            collective_id=0, has_side_effects=True, vmem_limit_bytes=64 * 1024 * 1024,
        ),
    )(attn_out, out_weight, residual, norm_gain.reshape(1, width), weights, w_gate, w_up, w_down)


def solution(mesh):
    in_specs = (
        P(("groups", "ctx"), "head"),
        P("head", "ctx"),
        P(("groups", "ctx", "head"), None),
        P(),
        P(("groups", "ctx", "head"), None),
        P(("groups", "ctx", "head"), None),
        P("ctx", None, "head"),
        P("ctx", None, "head"),
        P("ctx", "head", None),
    )
    out_specs = P(("groups", "ctx", "head"), None)
    whole_in_vmem = mesh.shape["ctx"] == 4 and mesh.shape["head"] == 4
    body = local_kernel if whole_in_vmem else local
    return jax.shard_map(body, mesh=mesh, in_specs=in_specs, out_specs=out_specs, check_vma=False)
```

```python
import jax
import jax.numpy as jnp
from jax import lax
from jax.experimental import pallas as pl
from jax.experimental.pallas import tpu as pltpu
from jax.sharding import PartitionSpec as P


def route_places(expert_ids, experts, capacity):
    flattened = expert_ids.reshape(-1)
    onehot = (flattened[:, None] == jnp.arange(experts, dtype=jnp.int32)[None, :]).astype(jnp.int32)
    before = jnp.cumsum(onehot, axis=0) - onehot
    slot_index = jnp.sum(onehot * before, axis=1)
    return (flattened * capacity + slot_index).reshape(expert_ids.shape)


def expert_apply(token_rows, w_gate, w_up, w_down):
    row_shape = token_rows.shape
    flattened = token_rows.reshape(-1, row_shape[-1])
    gate_proj = jnp.dot(flattened, w_gate[0], preferred_element_type=jnp.float32)
    up_proj = jnp.dot(flattened, w_up[0], preferred_element_type=jnp.float32)
    activation = (jax.nn.silu(gate_proj) * up_proj).astype(jnp.bfloat16)
    result = jnp.dot(activation, w_down[0], preferred_element_type=jnp.float32)
    return result.reshape(row_shape)


def local(attn_out, out_weight, residual, norm_gain, expert_ids, gate_codes, w_gate, w_up, w_down):
    ctx_count = lax.axis_size("ctx")
    rows_dev = residual.shape[0]
    model_width = residual.shape[1]
    partial_sums = jnp.dot(
        attn_out,
        lax.all_gather(out_weight, "ctx", axis=1, tiled=True),
        preferred_element_type=jnp.float32,
    )
    projected = lax.psum_scatter(
        partial_sums.astype(jnp.bfloat16), "head", scatter_dimension=0, tiled=True
    ).astype(jnp.float32)
    hidden_state = residual.astype(jnp.float32) + projected
    mean_square = jnp.mean(hidden_state * hidden_state, axis=1, keepdims=True)
    normed = (hidden_state * lax.rsqrt(mean_square + 1e-06) * norm_gain).astype(jnp.bfloat16)
    routes = expert_ids.shape[1]
    capacity = min(rows_dev, max(2, (3 * rows_dev * routes + 2 * ctx_count - 1) // (2 * ctx_count)))
    places = route_places(expert_ids, ctx_count, capacity)
    slot_range = jnp.arange(ctx_count * capacity, dtype=jnp.int32)
    select = jnp.any(slot_range[:, None, None] == places[None, :, :], axis=2).astype(jnp.bfloat16)
    outbound = jnp.dot(select, normed, preferred_element_type=jnp.float32).astype(jnp.bfloat16)
    outbound = outbound.reshape(ctx_count, capacity, model_width)
    arrived = lax.all_to_all(outbound, "ctx", split_axis=0, concat_axis=0, tiled=True)
    partial_out = expert_apply(
        lax.all_gather(arrived[:, None], "head", axis=1, tiled=True), w_gate, w_up, w_down
    )
    summed_out = lax.psum_scatter(
        partial_out.astype(jnp.bfloat16), "head", scatter_dimension=1, tiled=True
    ).astype(jnp.float32)
    returned = lax.all_to_all(
        summed_out.reshape(ctx_count, capacity, model_width).astype(jnp.bfloat16),
        "ctx",
        split_axis=0,
        concat_axis=0,
        tiled=True,
    ).astype(jnp.float32)
    gate_values = gate_codes.astype(jnp.float32)
    route_weights = 2.5 * gate_values / jnp.sum(gate_values, axis=1, keepdims=True)
    matching = places[:, :, None] == slot_range[None, None, :]
    mixing = jnp.sum(jnp.where(matching, route_weights[:, :, None], 0.0), axis=1)
    combined = jnp.dot(
        mixing,
        returned.reshape(ctx_count * capacity, model_width),
        precision=lax.Precision.HIGHEST,
        preferred_element_type=jnp.float32,
    )
    return (hidden_state + combined).astype(jnp.bfloat16)


BF16, F32 = jnp.bfloat16, jnp.float32
SEMS = 72


def layer_kernel(
    attn, out_w, resid, gain, route_w, gate_w, up_w, down_w, out,
    attn_all, work, gate_v, up_v, down_v, res_cols, part, arrived, hidden, scaled,
    gate_acc, up_acc, square_sum, act, route_all, mine,
    core_in, core_x_in, head_in, last_out, last_in, send, recv, local_sem,
):
    c, h = lax.axis_index("ctx"), lax.axis_index("head")
    x, k = c // 2, c % 2
    rows = resid.shape[0]
    span, group = 4 * rows, 16 * rows
    cols = part.shape[2]
    tile = 256 if cols % 256 == 0 else 128
    tiles = cols // tile
    hidden_units = gate_acc.shape[1]

    ctx_of = [c, 2 * x + (1 - k), 2 * (1 - x) + k, 2 * (1 - x) + (1 - k)]
    to = [lax.rem(h + d, 4) for d in range(4)]
    source = [lax.rem(h + 4 - d, 4) for d in range(4)]
    SIB, ACROSS, DIAG = 1, 2, 3

    def at(start, size):
        return pl.ds(pl.multiple_of(start, size), size)

    def cols_at(start):
        return pl.ds(pl.multiple_of(start, 128), tile)

    def remote(src, dst, number, j=0, d=0, back=False):
        head = (source if back else to)[d]
        return pltpu.make_async_remote_copy(
            src_ref=src, dst_ref=dst, send_sem=send.at[number], recv_sem=recv.at[number],
            device_id={"ctx": ctx_of[j], "head": head}, device_id_type=pl.DeviceIdType.MESH,
        )

    started = []

    def push(src, dst, number, j=0, d=0):
        copy = remote(src, dst, number, j, d)
        copy.start()
        started.append(copy)

    def landed(dst, number, j=0, d=0):
        remote(dst, dst, number, j, d, back=True).wait_recv()

    barrier = pltpu.get_barrier_semaphore()
    for j in range(4):
        for d in range(4):
            if (j, d) != (0, 0):
                pl.semaphore_signal(
                    barrier, inc=1, device_id={"ctx": ctx_of[j], "head": to[d]},
                    device_id_type=pl.DeviceIdType.MESH,
                )

    depth = out_w.shape[0]
    own_copies = [
        pltpu.make_async_copy(attn, attn_all.at[c], local_sem.at[0]),
        pltpu.make_async_copy(out_w, work.at[pl.ds(0, depth)], local_sem.at[1]),
        pltpu.make_async_copy(resid.at[:, at(c * cols, cols)], res_cols.at[at(c * rows, rows)], local_sem.at[2]),
        pltpu.make_async_copy(gate_w.at[0], gate_v, local_sem.at[3]),
        pltpu.make_async_copy(up_w.at[0], up_v, local_sem.at[4]),
        pltpu.make_async_copy(down_w.at[0], down_v, local_sem.at[5]),
    ]
    for copy in own_copies[:3]:
        copy.start()
    pl.semaphore_wait(barrier, 15)

    push(attn, attn_all.at[c], 0, ACROSS)
    push(attn, attn_all.at[c], 1, SIB)
    for j in (1, 2, 3):
        push(resid.at[:, at(ctx_of[j] * cols, cols)], res_cols.at[at(c * rows, rows)], 2 + j, j)
    for j in range(4):
        for d in range(4):
            if (j, d) != (0, 0):
                push(route_w, route_all.at[at(h * span + c * rows, rows)], 6 + 4 * j + d - 1, j, d)
    route_all[at(h * span + c * rows, rows), :] = route_w[...]

    def project(j):
        block = ctx_of[j]

        def step(t, _):
            column = cols_at(t * tile)
            y = jnp.dot(attn_all[block], work[pl.ds(0, depth), column], preferred_element_type=F32).astype(BF16)
            for i in range(4):
                part[i, at(block * rows, rows), column] = y[i * rows:(i + 1) * rows]
            return 0

        lax.fori_loop(0, tiles, step, 0)
        for d in (2, 1, 3):
            place = at(block * rows, rows)
            push(part.at[to[d], place], arrived.at[d - 1, place], 21 + 3 * j + d - 1, 0, d)

    own_copies[0].wait()
    own_copies[1].wait()
    for copy in own_copies[3:]:
        copy.start()
    project(0)
    landed(attn_all.at[ctx_of[SIB]], 1, SIB)
    project(1)
    landed(attn_all.at[ctx_of[ACROSS]], 0, ACROSS)
    push(attn_all.at[ctx_of[ACROSS]], attn_all.at[ctx_of[ACROSS]], 2, SIB)
    project(2)
    landed(attn_all.at[ctx_of[DIAG]], 2, SIB)
    project(3)

    own_copies[2].wait()
    for j in (1, 2, 3):
        landed(res_cols.at[at(ctx_of[j] * rows, rows)], 2 + j, j)
    for j in range(4):
        for d in (1, 2, 3):
            landed(arrived.at[d - 1, at(ctx_of[j] * rows, rows)], 21 + 3 * j + d - 1, 0, d)

    def add_up(t, _):
        column = cols_at(t * tile)
        total = part[h, :, column].astype(F32) + res_cols[:, column].astype(F32)
        for d in range(3):
            total = total + arrived[d, :, column].astype(F32)
        hidden[c, at(h * span, span), column] = total.astype(BF16)
        return 0

    lax.fori_loop(0, tiles, add_up, 0)

    def block_of(j, b):
        return hidden.at[ctx_of[j], at(b * span, span)]

    def line(b, number, step):
        return pltpu.make_async_remote_copy(
            src_ref=block_of(0, b), dst_ref=block_of(0, b), send_sem=send.at[number], recv_sem=recv.at[number],
            device_id={"ctx": c, "head": h + step}, device_id_type=pl.DeviceIdType.MESH,
        )

    def pass_on(b):
        remote(block_of(0, b), block_of(0, b), 36 + b, ACROSS).start()
        remote(block_of(0, b), block_of(0, b), 40 + b, SIB).start()

    def streams(i):
        return ((h - i, h - i >= 0, h < 3, 33, 1), (h + i, h + i <= 3, h > 0, 67, -1))

    for b, there, onward, first, step in streams(0):
        pl.when(onward)(lambda b=b, first=first, step=step: line(b, first, step).start())
    pass_on(h)

    square_sum[...] = jnp.zeros_like(square_sum)
    gate_acc[...] = jnp.zeros_like(gate_acc)
    up_acc[...] = jnp.zeros_like(up_acc)
    for j in range(4):
        for d in range(4):
            if (j, d) != (0, 0):
                landed(route_all.at[at(source[d] * span + ctx_of[j] * rows, rows)], 6 + 4 * j + d - 1, j, d)
    lane = lax.broadcasted_iota(jnp.int32, route_all.shape, 1)
    mine[...] = jnp.sum(jnp.where(lane == c, route_all[...], 0.0), axis=1, keepdims=True)

    def expand(j):
        block = ctx_of[j]

        def scale(i, _):
            column = lax.rem(i, tiles)
            place = at((i // tiles) * span, span)
            value = hidden[block, place, cols_at(column * tile)].astype(F32)
            square_sum[place, :] += jnp.sum(value * value, axis=1, keepdims=True)
            g = gain[:, cols_at(block * cols + column * tile)]
            scaled[place, cols_at(column * tile)] = (value * g).astype(BF16)
            return 0

        lax.fori_loop(0, 4 * tiles, scale, 0)

        def step(t, _):
            unit = cols_at(t * tile)
            place = at(block * cols, cols)
            gate_acc[:, unit] += jnp.dot(scaled[...], gate_v[place, unit], preferred_element_type=F32)
            up_acc[:, unit] += jnp.dot(scaled[...], up_v[place, unit], preferred_element_type=F32)
            return 0

        lax.fori_loop(0, hidden_units // tile, step, 0)

    for i in (1, 2, 3):
        for b, there, onward, first, step in streams(i):

            @pl.when(there)
            def _():
                line(b, first + i - 1, -step).wait_recv()
                if i < 3:
                    pl.when(onward)(lambda: line(b, first + i, step).start())
                pass_on(b)

    def to_sibling(i):
        for b, there, onward, first, step in streams(i):

            @pl.when(there)
            def _():
                remote(block_of(ACROSS, b), block_of(ACROSS, b), 36 + b, ACROSS).wait_recv()
                remote(block_of(ACROSS, b), block_of(ACROSS, b), 44 + b, SIB).start()

    remote(block_of(ACROSS, h), block_of(ACROSS, h), 36 + h, ACROSS).wait_recv()
    remote(block_of(ACROSS, h), block_of(ACROSS, h), 44 + h, SIB).start()
    to_sibling(1)
    own_copies[3].wait()
    own_copies[4].wait()
    expand(0)
    for b in range(4):
        landed(block_of(SIB, b), 40 + b, SIB)
    to_sibling(2)
    expand(1)
    to_sibling(3)
    expand(2)
    for b in range(4):
        landed(block_of(DIAG, b), 44 + b, SIB)
    expand(3)

    def activate(i, _):
        place = at(i * rows, rows)
        r = lax.rsqrt(square_sum[place, :] * (1.0 / (4 * cols)) + 1e-06)
        g = gate_acc[place, :] * r
        act[place, :] = (g / (1.0 + jnp.exp(-g)) * (up_acc[place, :] * r)).astype(BF16)
        return 0

    lax.fori_loop(0, 16, activate, 0)
    own_copies[5].wait()

    def chunk(s, block):
        return (4 * s + block) * span

    def down(s):
        target = to[(s + 1) % 4]

        def half_of(core):
            def step(i, _):
                block, t = 2 * core + i // tiles, lax.rem(i, tiles)
                y = jnp.dot(
                    act[at(target * span, span), :], down_v[:, cols_at(block * cols + t * tile)],
                    preferred_element_type=F32,
                )
                y = y * mine[at(target * span, span), :]
                work[at(chunk(s, block), span), cols_at(t * tile)] = y.astype(BF16)
                return 0

            lax.fori_loop(0, 2 * tiles, step, 0)

        half_of(1 - k)
        push(work.at[pl.ds(pl.multiple_of(chunk(s, 2 * (1 - k)), span), 2 * span)], core_in.at[s], 48 + s, SIB)
        half_of(k)

    half = 2 * rows

    def over_x(s):
        landed(core_in.at[s], 48 + s, SIB)

        def step(i, _):
            j, t = i // tiles, lax.rem(i, tiles)
            place, column = at(chunk(s, 2 * k + j), span), cols_at(t * tile)
            y = work[place, column].astype(F32) + core_in[s, at(j * span, span), column].astype(F32)
            work[place, column] = y.astype(BF16)
            return 0

        lax.fori_loop(0, 2 * tiles, step, 0)
        for j in range(2):
            push(work.at[at(chunk(s, 2 * k + j) + (1 - x) * half, half)], core_x_in.at[s, j], 52 + 2 * s + j, ACROSS)

    def over_head(s):
        for j in range(2):
            landed(core_x_in.at[s, j], 52 + 2 * s + j, ACROSS)

        def step(i, _):
            j, t = i // tiles, lax.rem(i, tiles)
            place, column = at(chunk(s, 2 * k + j) + x * half, half), cols_at(t * tile)
            y = work[place, column].astype(F32) + core_x_in[s, j, :, column].astype(F32)
            work[place, column] = y.astype(BF16)
            return 0

        lax.fori_loop(0, 2 * tiles, step, 0)
        if s < 3:
            for j in range(2):
                push(work.at[at(chunk(s, 2 * k + j) + x * half, half)], head_in.at[s, j], 60 + 2 * s + j, 0, s + 1)

    for s in range(4):
        down(s)
        over_x(s)
    for s in range(4):
        over_head(s)
    for s in range(3):
        for j in range(2):
            landed(head_in.at[s, j], 60 + 2 * s + j, 0, s + 1)

    def total(core, i):
        j, t = i // tiles, lax.rem(i, tiles)
        column = cols_at(t * tile)
        y = work[at(chunk(3, 2 * k + j) + x * half + core * rows, rows), column].astype(F32)
        for s in range(3):
            y = y + head_in[s, j, at(core * rows, rows), column].astype(F32)
        return y

    def other(i, _):
        last_out[i // tiles, :, cols_at(lax.rem(i, tiles) * tile)] = total(1 - k, i).astype(BF16)
        return 0

    lax.fori_loop(0, 2 * tiles, other, 0)
    push(last_out, last_in, 66, SIB)

    def finish(block, i, y):
        t = lax.rem(i, tiles)
        kept = hidden[block, at(h * span + c * rows, rows), cols_at(t * tile)].astype(F32)
        out[:, cols_at(block * cols + t * tile)] = (kept + y).astype(BF16)

    def own(i, _):
        finish(2 * k + i // tiles, i, total(k, i))
        return 0

    lax.fori_loop(0, 2 * tiles, own, 0)
    landed(last_in, 66, SIB)

    def theirs(i, _):
        y = last_in[i // tiles, :, cols_at(lax.rem(i, tiles) * tile)].astype(F32)
        finish(2 * (1 - k) + i // tiles, i, y)
        return 0

    lax.fori_loop(0, 2 * tiles, theirs, 0)
    for copy in started:
        copy.wait_send()
    for b in range(4):
        remote(block_of(0, b), block_of(0, b), 36 + b, ACROSS).wait_send()
        remote(block_of(0, b), block_of(0, b), 40 + b, SIB).wait_send()
        remote(block_of(ACROSS, b), block_of(ACROSS, b), 44 + b, SIB).wait_send()
    for i in range(3):
        for b, there, onward, first, step in streams(i):
            pl.when(there & onward)(lambda: line(b, first + i, step).wait_send())


def local_kernel(attn_out, out_weight, residual, norm_gain, expert_ids, gate_codes, w_gate, w_up, w_down):
    rows, width = residual.shape
    depth, cols = out_weight.shape
    units = w_gate.shape[2]
    gate_values = gate_codes.astype(F32)
    route_weights = 2.5 * gate_values / jnp.sum(gate_values, axis=1, keepdims=True)
    named = expert_ids[:, :, None] == jnp.arange(128, dtype=jnp.int32)
    weights = jnp.sum(jnp.where(named, route_weights[:, :, None], 0.0), axis=1)
    span, group = 4 * rows, 16 * rows
    vmem, hbm = pl.BlockSpec(memory_space=pltpu.VMEM), pl.BlockSpec(memory_space=pl.ANY)
    return pl.pallas_call(
        layer_kernel,
        out_shape=jax.ShapeDtypeStruct((rows, width), BF16),
        in_specs=[hbm, hbm, hbm, vmem, vmem, hbm, hbm, hbm],
        out_specs=vmem,
        scratch_shapes=[
            pltpu.VMEM((4, span, depth), BF16),
            pltpu.VMEM((max(depth, 16 * span), cols), BF16),
            pltpu.VMEM((width, units), BF16),
            pltpu.VMEM((width, units), BF16),
            pltpu.VMEM((units, width), BF16),
            pltpu.VMEM((span, cols), BF16),
            pltpu.VMEM((4, span, cols), BF16),
            pltpu.VMEM((3, span, cols), BF16),
            pltpu.VMEM((4, group, cols), BF16),
            pltpu.VMEM((group, cols), BF16),
            pltpu.VMEM((group, units), F32),
            pltpu.VMEM((group, units), F32),
            pltpu.VMEM((group, 1), F32),
            pltpu.VMEM((group, units), BF16),
            pltpu.VMEM((group, 128), F32),
            pltpu.VMEM((group, 1), F32),
            pltpu.VMEM((4, 2 * span, cols), BF16),
            pltpu.VMEM((4, 2, 2 * rows, cols), BF16),
            pltpu.VMEM((3, 2, 2 * rows, cols), BF16),
            pltpu.VMEM((2, rows, cols), BF16),
            pltpu.VMEM((2, rows, cols), BF16),
            pltpu.SemaphoreType.DMA((SEMS,)),
            pltpu.SemaphoreType.DMA((SEMS,)),
            pltpu.SemaphoreType.DMA((6,)),
        ],
        compiler_params=pltpu.CompilerParams(
            collective_id=0, has_side_effects=True, vmem_limit_bytes=64 * 1024 * 1024,
        ),
    )(attn_out, out_weight, residual, norm_gain.reshape(1, width), weights, w_gate, w_up, w_down)


def solution(mesh):
    in_specs = (
        P(("groups", "ctx"), "head"),
        P("head", "ctx"),
        P(("groups", "ctx", "head"), None),
        P(),
        P(("groups", "ctx", "head"), None),
        P(("groups", "ctx", "head"), None),
        P("ctx", None, "head"),
        P("ctx", None, "head"),
        P("ctx", "head", None),
    )
    out_specs = P(("groups", "ctx", "head"), None)
    whole_in_vmem = mesh.shape["ctx"] == 4 and mesh.shape["head"] == 4
    body = local_kernel if whole_in_vmem else local
    return jax.shard_map(body, mesh=mesh, in_specs=in_specs, out_specs=out_specs, check_vma=False)
```

```python
import jax
import jax.numpy as jnp
from jax import lax
from jax.experimental import pallas as pl
from jax.experimental.pallas import tpu as pltpu
from jax.sharding import PartitionSpec as P


def route_places(expert_ids, experts, capacity):
    flattened = expert_ids.reshape(-1)
    onehot = (flattened[:, None] == jnp.arange(experts, dtype=jnp.int32)[None, :]).astype(jnp.int32)
    before = jnp.cumsum(onehot, axis=0) - onehot
    slot_index = jnp.sum(onehot * before, axis=1)
    return (flattened * capacity + slot_index).reshape(expert_ids.shape)


def expert_apply(token_rows, w_gate, w_up, w_down):
    row_shape = token_rows.shape
    flattened = token_rows.reshape(-1, row_shape[-1])
    gate_proj = jnp.dot(flattened, w_gate[0], preferred_element_type=jnp.float32)
    up_proj = jnp.dot(flattened, w_up[0], preferred_element_type=jnp.float32)
    activation = (jax.nn.silu(gate_proj) * up_proj).astype(jnp.bfloat16)
    result = jnp.dot(activation, w_down[0], preferred_element_type=jnp.float32)
    return result.reshape(row_shape)


def local(attn_out, out_weight, residual, norm_gain, expert_ids, gate_codes, w_gate, w_up, w_down):
    ctx_count = lax.axis_size("ctx")
    rows_dev = residual.shape[0]
    model_width = residual.shape[1]
    partial_sums = jnp.dot(
        attn_out,
        lax.all_gather(out_weight, "ctx", axis=1, tiled=True),
        preferred_element_type=jnp.float32,
    )
    projected = lax.psum_scatter(
        partial_sums.astype(jnp.bfloat16), "head", scatter_dimension=0, tiled=True
    ).astype(jnp.float32)
    hidden_state = residual.astype(jnp.float32) + projected
    mean_square = jnp.mean(hidden_state * hidden_state, axis=1, keepdims=True)
    normed = (hidden_state * lax.rsqrt(mean_square + 1e-06) * norm_gain).astype(jnp.bfloat16)
    routes = expert_ids.shape[1]
    capacity = min(rows_dev, max(2, (3 * rows_dev * routes + 2 * ctx_count - 1) // (2 * ctx_count)))
    places = route_places(expert_ids, ctx_count, capacity)
    slot_range = jnp.arange(ctx_count * capacity, dtype=jnp.int32)
    select = jnp.any(slot_range[:, None, None] == places[None, :, :], axis=2).astype(jnp.bfloat16)
    outbound = jnp.dot(select, normed, preferred_element_type=jnp.float32).astype(jnp.bfloat16)
    outbound = outbound.reshape(ctx_count, capacity, model_width)
    arrived = lax.all_to_all(outbound, "ctx", split_axis=0, concat_axis=0, tiled=True)
    partial_out = expert_apply(
        lax.all_gather(arrived[:, None], "head", axis=1, tiled=True), w_gate, w_up, w_down
    )
    summed_out = lax.psum_scatter(
        partial_out.astype(jnp.bfloat16), "head", scatter_dimension=1, tiled=True
    ).astype(jnp.float32)
    returned = lax.all_to_all(
        summed_out.reshape(ctx_count, capacity, model_width).astype(jnp.bfloat16),
        "ctx",
        split_axis=0,
        concat_axis=0,
        tiled=True,
    ).astype(jnp.float32)
    gate_values = gate_codes.astype(jnp.float32)
    route_weights = 2.5 * gate_values / jnp.sum(gate_values, axis=1, keepdims=True)
    matching = places[:, :, None] == slot_range[None, None, :]
    mixing = jnp.sum(jnp.where(matching, route_weights[:, :, None], 0.0), axis=1)
    combined = jnp.dot(
        mixing,
        returned.reshape(ctx_count * capacity, model_width),
        precision=lax.Precision.HIGHEST,
        preferred_element_type=jnp.float32,
    )
    return (hidden_state + combined).astype(jnp.bfloat16)


BF16, F32 = jnp.bfloat16, jnp.float32
SEMS = 72


def layer_kernel(
    attn, out_w, resid, gain, route_w, gate_w, up_w, down_w, out,
    attn_all, work, gate_v, up_v, down_v, res_cols, part, arrived, hidden, scaled,
    gate_acc, up_acc, square_sum, act, route_all, mine,
    core_in, core_x_in, head_in, last_out, last_in, send, recv, local_sem,
):
    c, h = lax.axis_index("ctx"), lax.axis_index("head")
    x, k = c // 2, c % 2
    rows = resid.shape[0]
    span, group = 4 * rows, 16 * rows
    cols = part.shape[2]
    tile = 256 if cols % 256 == 0 else 128
    tiles = cols // tile
    hidden_units = gate_acc.shape[1]

    ctx_of = [c, 2 * x + (1 - k), 2 * (1 - x) + k, 2 * (1 - x) + (1 - k)]
    to = [lax.rem(h + d, 4) for d in range(4)]
    source = [lax.rem(h + 4 - d, 4) for d in range(4)]
    SIB, ACROSS, DIAG = 1, 2, 3

    def at(start, size):
        return pl.ds(pl.multiple_of(start, size), size)

    def cols_at(start):
        return pl.ds(pl.multiple_of(start, 128), tile)

    def remote(src, dst, number, j=0, d=0, back=False):
        head = (source if back else to)[d]
        return pltpu.make_async_remote_copy(
            src_ref=src, dst_ref=dst, send_sem=send.at[number], recv_sem=recv.at[number],
            device_id={"ctx": ctx_of[j], "head": head}, device_id_type=pl.DeviceIdType.MESH,
        )

    started = []

    def push(src, dst, number, j=0, d=0):
        copy = remote(src, dst, number, j, d)
        copy.start()
        started.append(copy)

    def landed(dst, number, j=0, d=0):
        remote(dst, dst, number, j, d, back=True).wait_recv()

    barrier = pltpu.get_barrier_semaphore()
    for j in range(4):
        for d in range(4):
            if (j, d) != (0, 0):
                pl.semaphore_signal(
                    barrier, inc=1, device_id={"ctx": ctx_of[j], "head": to[d]},
                    device_id_type=pl.DeviceIdType.MESH,
                )

    depth = out_w.shape[0]
    own_copies = [
        pltpu.make_async_copy(attn, attn_all.at[c], local_sem.at[0]),
        pltpu.make_async_copy(out_w, work.at[pl.ds(0, depth)], local_sem.at[1]),
        pltpu.make_async_copy(resid.at[:, at(c * cols, cols)], res_cols.at[at(c * rows, rows)], local_sem.at[2]),
        pltpu.make_async_copy(gate_w.at[0], gate_v, local_sem.at[3]),
        pltpu.make_async_copy(up_w.at[0], up_v, local_sem.at[4]),
        pltpu.make_async_copy(down_w.at[0], down_v, local_sem.at[5]),
    ]
    for copy in own_copies[:3]:
        copy.start()
    pl.semaphore_wait(barrier, 15)

    push(attn, attn_all.at[c], 0, ACROSS)
    push(attn, attn_all.at[c], 1, SIB)
    for j in (1, 2, 3):
        push(resid.at[:, at(ctx_of[j] * cols, cols)], res_cols.at[at(c * rows, rows)], 2 + j, j)
    for j in range(4):
        for d in range(4):
            if (j, d) != (0, 0):
                push(route_w, route_all.at[at(h * span + c * rows, rows)], 6 + 4 * j + d - 1, j, d)
    route_all[at(h * span + c * rows, rows), :] = route_w[...]

    def project(j):
        block = ctx_of[j]

        def step(t, _):
            column = cols_at(t * tile)
            y = jnp.dot(attn_all[block], work[pl.ds(0, depth), column], preferred_element_type=F32).astype(BF16)
            for i in range(4):
                part[i, at(block * rows, rows), column] = y[i * rows:(i + 1) * rows]
            return 0

        lax.fori_loop(0, tiles, step, 0)
        for d in (2, 1, 3):
            place = at(block * rows, rows)
            push(part.at[to[d], place], arrived.at[d - 1, place], 21 + 3 * j + d - 1, 0, d)

    own_copies[0].wait()
    own_copies[1].wait()
    for copy in own_copies[3:]:
        copy.start()
    project(0)
    landed(attn_all.at[ctx_of[SIB]], 1, SIB)
    project(1)
    landed(attn_all.at[ctx_of[ACROSS]], 0, ACROSS)
    push(attn_all.at[ctx_of[ACROSS]], attn_all.at[ctx_of[ACROSS]], 2, SIB)
    project(2)
    landed(attn_all.at[ctx_of[DIAG]], 2, SIB)
    project(3)

    own_copies[2].wait()
    for j in (1, 2, 3):
        landed(res_cols.at[at(ctx_of[j] * rows, rows)], 2 + j, j)
    for j in range(4):
        for d in (1, 2, 3):
            landed(arrived.at[d - 1, at(ctx_of[j] * rows, rows)], 21 + 3 * j + d - 1, 0, d)

    def add_up(t, _):
        column = cols_at(t * tile)
        total = part[h, :, column].astype(F32) + res_cols[:, column].astype(F32)
        for d in range(3):
            total = total + arrived[d, :, column].astype(F32)
        hidden[c, at(h * span, span), column] = total.astype(BF16)
        return 0

    lax.fori_loop(0, tiles, add_up, 0)

    def block_of(j, b):
        return hidden.at[ctx_of[j], at(b * span, span)]

    def line(b, number, step):
        return pltpu.make_async_remote_copy(
            src_ref=block_of(0, b), dst_ref=block_of(0, b), send_sem=send.at[number], recv_sem=recv.at[number],
            device_id={"ctx": c, "head": h + step}, device_id_type=pl.DeviceIdType.MESH,
        )

    def pass_on(b):
        remote(block_of(0, b), block_of(0, b), 36 + b, ACROSS).start()
        remote(block_of(0, b), block_of(0, b), 40 + b, SIB).start()

    def streams(i):
        return ((h - i, h - i >= 0, h < 3, 33, 1), (h + i, h + i <= 3, h > 0, 67, -1))

    for b, there, onward, first, step in streams(0):
        pl.when(onward)(lambda b=b, first=first, step=step: line(b, first, step).start())
    pass_on(h)

    square_sum[...] = jnp.zeros_like(square_sum)
    gate_acc[...] = jnp.zeros_like(gate_acc)
    up_acc[...] = jnp.zeros_like(up_acc)
    for j in range(4):
        for d in range(4):
            if (j, d) != (0, 0):
                landed(route_all.at[at(source[d] * span + ctx_of[j] * rows, rows)], 6 + 4 * j + d - 1, j, d)
    lane = lax.broadcasted_iota(jnp.int32, route_all.shape, 1)
    mine[...] = jnp.sum(jnp.where(lane == c, route_all[...], 0.0), axis=1, keepdims=True)

    def expand(j):
        block = ctx_of[j]

        def scale(i, _):
            column = lax.rem(i, tiles)
            place = at((i // tiles) * span, span)
            value = hidden[block, place, cols_at(column * tile)].astype(F32)
            square_sum[place, :] += jnp.sum(value * value, axis=1, keepdims=True)
            g = gain[:, cols_at(block * cols + column * tile)]
            scaled[place, cols_at(column * tile)] = (value * g).astype(BF16)
            return 0

        lax.fori_loop(0, 4 * tiles, scale, 0)

        def step(t, _):
            unit = cols_at(t * tile)
            place = at(block * cols, cols)
            gate_acc[:, unit] += jnp.dot(scaled[...], gate_v[place, unit], preferred_element_type=F32)
            up_acc[:, unit] += jnp.dot(scaled[...], up_v[place, unit], preferred_element_type=F32)
            return 0

        lax.fori_loop(0, hidden_units // tile, step, 0)

    for i in (1, 2, 3):
        for b, there, onward, first, step in streams(i):

            @pl.when(there)
            def _():
                line(b, first + i - 1, -step).wait_recv()
                if i < 3:
                    pl.when(onward)(lambda: line(b, first + i, step).start())
                pass_on(b)

    def to_sibling(i):
        for b, there, onward, first, step in streams(i):

            @pl.when(there)
            def _():
                remote(block_of(ACROSS, b), block_of(ACROSS, b), 36 + b, ACROSS).wait_recv()
                remote(block_of(ACROSS, b), block_of(ACROSS, b), 44 + b, SIB).start()

    remote(block_of(ACROSS, h), block_of(ACROSS, h), 36 + h, ACROSS).wait_recv()
    remote(block_of(ACROSS, h), block_of(ACROSS, h), 44 + h, SIB).start()
    to_sibling(1)
    own_copies[3].wait()
    own_copies[4].wait()
    expand(0)
    for b in range(4):
        landed(block_of(SIB, b), 40 + b, SIB)
    to_sibling(2)
    expand(1)
    to_sibling(3)
    expand(2)
    for b in range(4):
        landed(block_of(DIAG, b), 44 + b, SIB)
    expand(3)

    def activate(i, _):
        place = at(i * rows, rows)
        r = lax.rsqrt(square_sum[place, :] * (1.0 / (4 * cols)) + 1e-06)
        g = gate_acc[place, :] * r
        act[place, :] = (g / (1.0 + jnp.exp(-g)) * (up_acc[place, :] * r)).astype(BF16)
        return 0

    lax.fori_loop(0, 16, activate, 0)
    own_copies[5].wait()

    def chunk(s, block):
        return (4 * s + block) * span

    def down(s):
        target = to[(s + 1) % 4]

        def half_of(core):
            def step(i, _):
                block, t = 2 * core + i // tiles, lax.rem(i, tiles)
                y = jnp.dot(
                    act[at(target * span, span), :], down_v[:, cols_at(block * cols + t * tile)],
                    preferred_element_type=F32,
                )
                y = y * mine[at(target * span, span), :]
                work[at(chunk(s, block), span), cols_at(t * tile)] = y.astype(BF16)
                return 0

            lax.fori_loop(0, 2 * tiles, step, 0)

        half_of(1 - k)
        push(work.at[pl.ds(pl.multiple_of(chunk(s, 2 * (1 - k)), span), 2 * span)], core_in.at[s], 48 + s, SIB)
        half_of(k)

    half = 2 * rows

    def over_x(s):
        landed(core_in.at[s], 48 + s, SIB)

        def step(i, _):
            j, t = i // tiles, lax.rem(i, tiles)
            place, column = at(chunk(s, 2 * k + j), span), cols_at(t * tile)
            y = work[place, column].astype(F32) + core_in[s, at(j * span, span), column].astype(F32)
            work[place, column] = y.astype(BF16)
            return 0

        lax.fori_loop(0, 2 * tiles, step, 0)
        for j in range(2):
            push(work.at[at(chunk(s, 2 * k + j) + (1 - x) * half, half)], core_x_in.at[s, j], 52 + 2 * s + j, ACROSS)

    def over_head(s):
        for j in range(2):
            landed(core_x_in.at[s, j], 52 + 2 * s + j, ACROSS)

        def step(i, _):
            j, t = i // tiles, lax.rem(i, tiles)
            place, column = at(chunk(s, 2 * k + j) + x * half, half), cols_at(t * tile)
            y = work[place, column].astype(F32) + core_x_in[s, j, :, column].astype(F32)
            work[place, column] = y.astype(BF16)
            return 0

        lax.fori_loop(0, 2 * tiles, step, 0)
        if s < 3:
            for j in range(2):
                push(work.at[at(chunk(s, 2 * k + j) + x * half, half)], head_in.at[s, j], 60 + 2 * s + j, 0, s + 1)

    for s in range(4):
        down(s)
        if s:
            over_x(s - 1)
    over_x(3)
    for s in range(4):
        over_head(s)
    for s in range(3):
        for j in range(2):
            landed(head_in.at[s, j], 60 + 2 * s + j, 0, s + 1)

    def total(core, i):
        j, t = i // tiles, lax.rem(i, tiles)
        column = cols_at(t * tile)
        y = work[at(chunk(3, 2 * k + j) + x * half + core * rows, rows), column].astype(F32)
        for s in range(3):
            y = y + head_in[s, j, at(core * rows, rows), column].astype(F32)
        return y

    def other(i, _):
        last_out[i // tiles, :, cols_at(lax.rem(i, tiles) * tile)] = total(1 - k, i).astype(BF16)
        return 0

    lax.fori_loop(0, 2 * tiles, other, 0)
    push(last_out, last_in, 66, SIB)

    def finish(block, i, y):
        t = lax.rem(i, tiles)
        kept = hidden[block, at(h * span + c * rows, rows), cols_at(t * tile)].astype(F32)
        out[:, cols_at(block * cols + t * tile)] = (kept + y).astype(BF16)

    def own(i, _):
        finish(2 * k + i // tiles, i, total(k, i))
        return 0

    lax.fori_loop(0, 2 * tiles, own, 0)
    landed(last_in, 66, SIB)

    def theirs(i, _):
        y = last_in[i // tiles, :, cols_at(lax.rem(i, tiles) * tile)].astype(F32)
        finish(2 * (1 - k) + i // tiles, i, y)
        return 0

    lax.fori_loop(0, 2 * tiles, theirs, 0)
    for copy in started:
        copy.wait_send()
    for b in range(4):
        remote(block_of(0, b), block_of(0, b), 36 + b, ACROSS).wait_send()
        remote(block_of(0, b), block_of(0, b), 40 + b, SIB).wait_send()
        remote(block_of(ACROSS, b), block_of(ACROSS, b), 44 + b, SIB).wait_send()
    for i in range(3):
        for b, there, onward, first, step in streams(i):
            pl.when(there & onward)(lambda: line(b, first + i, step).wait_send())


def local_kernel(attn_out, out_weight, residual, norm_gain, expert_ids, gate_codes, w_gate, w_up, w_down):
    rows, width = residual.shape
    depth, cols = out_weight.shape
    units = w_gate.shape[2]
    gate_values = gate_codes.astype(F32)
    route_weights = 2.5 * gate_values / jnp.sum(gate_values, axis=1, keepdims=True)
    named = expert_ids[:, :, None] == jnp.arange(128, dtype=jnp.int32)
    weights = jnp.sum(jnp.where(named, route_weights[:, :, None], 0.0), axis=1)
    span, group = 4 * rows, 16 * rows
    vmem, hbm = pl.BlockSpec(memory_space=pltpu.VMEM), pl.BlockSpec(memory_space=pl.ANY)
    return pl.pallas_call(
        layer_kernel,
        out_shape=jax.ShapeDtypeStruct((rows, width), BF16),
        in_specs=[hbm, hbm, hbm, vmem, vmem, hbm, hbm, hbm],
        out_specs=vmem,
        scratch_shapes=[
            pltpu.VMEM((4, span, depth), BF16),
            pltpu.VMEM((max(depth, 16 * span), cols), BF16),
            pltpu.VMEM((width, units), BF16),
            pltpu.VMEM((width, units), BF16),
            pltpu.VMEM((units, width), BF16),
            pltpu.VMEM((span, cols), BF16),
            pltpu.VMEM((4, span, cols), BF16),
            pltpu.VMEM((3, span, cols), BF16),
            pltpu.VMEM((4, group, cols), BF16),
            pltpu.VMEM((group, cols), BF16),
            pltpu.VMEM((group, units), F32),
            pltpu.VMEM((group, units), F32),
            pltpu.VMEM((group, 1), F32),
            pltpu.VMEM((group, units), BF16),
            pltpu.VMEM((group, 128), F32),
            pltpu.VMEM((group, 1), F32),
            pltpu.VMEM((4, 2 * span, cols), BF16),
            pltpu.VMEM((4, 2, 2 * rows, cols), BF16),
            pltpu.VMEM((3, 2, 2 * rows, cols), BF16),
            pltpu.VMEM((2, rows, cols), BF16),
            pltpu.VMEM((2, rows, cols), BF16),
            pltpu.SemaphoreType.DMA((SEMS,)),
            pltpu.SemaphoreType.DMA((SEMS,)),
            pltpu.SemaphoreType.DMA((6,)),
        ],
        compiler_params=pltpu.CompilerParams(
            collective_id=0, has_side_effects=True, vmem_limit_bytes=64 * 1024 * 1024,
        ),
    )(attn_out, out_weight, residual, norm_gain.reshape(1, width), weights, w_gate, w_up, w_down)


def solution(mesh):
    in_specs = (
        P(("groups", "ctx"), "head"),
        P("head", "ctx"),
        P(("groups", "ctx", "head"), None),
        P(),
        P(("groups", "ctx", "head"), None),
        P(("groups", "ctx", "head"), None),
        P("ctx", None, "head"),
        P("ctx", None, "head"),
        P("ctx", "head", None),
    )
    out_specs = P(("groups", "ctx", "head"), None)
    whole_in_vmem = mesh.shape["ctx"] == 4 and mesh.shape["head"] == 4
    body = local_kernel if whole_in_vmem else local
    return jax.shard_map(body, mesh=mesh, in_specs=in_specs, out_specs=out_specs, check_vma=False)
```
